32 devices in a mesh: dp: 4 (over x, core), fsdp: 8 (over z, y).
Axes of the slice: x: 2, y: 2, z: 4, core: 2. Of those that a mesh axis runs over, the one named last changes fastest.
Arguments:
- tokens: bfloat16 [1024, 4096], P(('dp', 'fsdp')), may hold values from -6 to 6
- cotangent: bfloat16 [1024, 4096], P(('dp', 'fsdp')), may hold values from -2 to 2
- gate_base: bfloat16 [4096, 10240], P(None, 'fsdp'), may hold values from -0.09375 to 0.09375
- up_base: bfloat16 [4096, 10240], P(None, 'fsdp'), may hold values from -0.09375 to 0.09375
- out_base: bfloat16 [10240, 4096], P('fsdp'), may hold values from -0.0625 to 0.0625
- subspace: float32 [512, 128], P('fsdp'), may hold values from -6 to 6
- sign_flips: int32 [2, 512, 128, 640], P(None, 'fsdp'), may hold values from -1 to 1, as said below
- fast_gains: bfloat16 [2, 512, 128, 640], P(None, None, 'fsdp'), may hold values from -5 to 5
- fast_scales: float32 [2, 512, 640], P(None, 'fsdp'), may hold values from 0.5 to 2
- block_orders: int32 [2, 512], replicated, may hold values from 0 to 511, each once within a row
Outputs:
- subspace_grad: float32 [512, 128], P('fsdp')
The draws below stay inside these ranges and needn't reach their ends.
Inputs may be any that keep to these rules, and one draw needn't show every extreme that they name: `sign_flips`: each entry is -1 or +1.
All inputs are finite; a program needn't handle non-finite values.
Results may differ from the reference program's by a relative error of at most 0.017.
Values may be sent and summed in bfloat16 or wider, within the bound.
A program may use at most 384 MiB of HBM per device.

```python
import math
import jax
import jax.numpy as jnp
from jax import lax

D = 4096
FF = 10240
HB = 128
NB = 512
ROWS = 256
BLOCKS = 640
N_DP = 4
N_FSDP = 8


def draw_sign_flips(key, part):
    key = jax.random.fold_in(key, 7)
    flips = jax.random.randint(key, (2, NB, HB, BLOCKS), 0, 2)
    return (2 * flips - 1).astype(jnp.int32)


def shard_levels(stream_key, shape, split, least, largest):
    loudness, own = 1.0, jax.random.fold_in(stream_key, 6)
    for axis_at, blocks in split:
        heights = jnp.exp(jax.random.uniform(jax.random.fold_in(own, axis_at), (blocks,), jnp.float32, least / len(split), largest / len(split)))
        loudness = loudness * jnp.repeat(heights, shape[axis_at] // blocks).reshape([-1 if axis == axis_at else 1 for axis in range(len(shape))])
    return loudness


def noise(own_key, shape, deviation, limit, pieces=(), kind=jnp.bfloat16):
    entries = deviation * jax.random.normal(own_key, shape, jnp.float32)
    if pieces:
        entries = entries * shard_levels(own_key, shape, pieces, -0.22, 0.18)
    return jnp.clip(entries, -limit, limit).astype(kind)


def setup_inputs(seed: int = 0) -> dict:
    seeds = jax.random.split(jax.random.key(seed), 11)
    return {
        "tokens": noise(seeds[0], (N_DP * ROWS, D), 1.0, 6.0, ((0, 32),)),
        "cotangent": noise(seeds[1], (N_DP * ROWS, D), (4.0 * (N_DP * ROWS) ** -0.5), 2.0, ((0, 32),)),
        "gate_base": noise(seeds[2], (D, FF), D ** -0.5, 0.09375, ((1, 8),)),
        "up_base": noise(seeds[3], (D, FF), D ** -0.5, 0.09375, ((1, 8),)),
        "out_base": noise(seeds[4], (FF, D), FF ** -0.5, 0.0625, ((0, 8),)),
        "subspace": noise(seeds[5], (NB, HB), 1.0, 6.0, ((0, 8),), jnp.float32),
        "sign_flips": draw_sign_flips(jax.random.fold_in(seeds[10], 71), 0),
        "fast_gains": noise(seeds[7], (2, NB, HB, BLOCKS), 1.0, 5.0, ((2, 8),)),
        "fast_scales": jnp.clip(jnp.exp(math.log(2.0) - 1.3862944 * jax.random.uniform(seeds[8], (2, NB, BLOCKS), jnp.float32) ** shard_levels(seeds[8], (2, NB, BLOCKS), ((1, 8),), -0.2, 0.2)), 0.5, 2.0),
        "block_orders": jax.vmap(lambda own: jax.random.permutation(own, NB))(jax.random.split(seeds[9], 2)).reshape((2, NB)).astype(jnp.int32),
    }


def hadamard(size, dtype):
    index = jnp.arange(size, dtype=jnp.int32)
    anded = jnp.bitwise_and(index[:, None], index[None, :])
    parity = jnp.zeros((size, size), jnp.int32)
    for bit in range(max(size.bit_length() - 1, 0)):
        parity = jnp.bitwise_xor(parity, jnp.bitwise_and(jnp.right_shift(anded, bit), 1))
    return (1 - 2 * parity).astype(dtype)


def gelu_tanh(value):
    argument = 0.7978845608028654 * (value + 0.044715 * value * value * value)
    return 0.5 * value * (1.0 + jnp.tanh(argument))


def gelu_slope(value):
    argument = 0.7978845608028654 * (value + 0.044715 * value * value * value)
    tangent = jnp.tanh(argument)
    return 0.5 * (1.0 + tangent) + 0.5 * value * (1.0 - tangent * tangent) * 0.7978845608028654 * (1.0 + 0.134145 * value * value)


def expand(signs, subspace, gains, scales, order, factor, parts):
    nb, hb, blocks = signs.shape
    inner = nb // parts
    highest = lax.Precision.HIGHEST
    lifted = signs.astype(jnp.float32) * subspace[:, :, None]
    grouped = lifted.reshape(parts, inner, hb, blocks)
    grouped = jnp.einsum('dc,pack->padk', hadamard(hb, jnp.float32), grouped, precision=highest)
    grouped = jnp.einsum('ba,pack->pbck', hadamard(inner, jnp.float32), grouped, precision=highest)
    first = (grouped * (inner * hb) ** -0.5).astype(jnp.bfloat16)
    turned = jnp.einsum('qp,pack->qack', hadamard(parts, jnp.float32), first.astype(jnp.float32), precision=highest) * parts ** -0.5
    turned = turned.reshape(nb, hb, blocks)
    mixed = (gains.astype(jnp.float32) * turned[order]).astype(jnp.bfloat16)
    second = jnp.einsum('cb,bxk->cxk', hadamard(nb, jnp.float32), mixed.astype(jnp.float32), precision=highest)
    second = (second * nb ** -0.5).astype(jnp.bfloat16)
    wide = jnp.einsum('dc,bck->bdk', hadamard(hb, jnp.float32), second.astype(jnp.float32), precision=highest)
    return wide * (scales[:, None, :] * (factor * hb ** -0.5))


def adjoint(grads, signs, gains, scales, order, factor, parts):
    nb, hb, blocks = signs.shape
    inner = nb // parts
    highest = lax.Precision.HIGHEST
    scaled = grads * (scales[:, None, :] * (factor * hb ** -0.5))
    back = jnp.einsum('dc,bck->bdk', hadamard(hb, jnp.float32), scaled, precision=highest).astype(jnp.bfloat16)
    spread = jnp.einsum('cb,bxk->cxk', hadamard(nb, jnp.float32), back.astype(jnp.float32), precision=highest) * nb ** -0.5
    spread = (gains.astype(jnp.float32) * spread).astype(jnp.bfloat16)
    inverse = jnp.zeros((nb,), jnp.int32).at[order].set(jnp.arange(nb, dtype=jnp.int32))
    reverted = spread[inverse].reshape(parts, inner, hb, blocks)
    folded = jnp.einsum('qp,pack->qack', hadamard(parts, jnp.float32), reverted.astype(jnp.float32), precision=highest) * parts ** -0.5
    folded = folded.astype(jnp.bfloat16)
    wide = jnp.einsum('dc,pack->padk', hadamard(hb, jnp.float32), folded.astype(jnp.float32), precision=highest)
    wide = jnp.einsum('ba,pack->pbck', hadamard(inner, jnp.float32), wide, precision=highest) * (inner * hb) ** -0.5
    return jnp.sum(signs.astype(jnp.float32) * wide.reshape(nb, hb, blocks), axis=2)


def contract(left, right, left_dim, right_dim):
    return lax.dot_general(left, right, (((left_dim,), (right_dim,)), ((), ())), preferred_element_type=jnp.float32)


def reference(tokens, cotangent, gate_base, up_base, out_base, subspace, sign_flips, fast_gains, fast_scales, block_orders):
    parts = N_FSDP
    factors = (D ** -0.5, FF ** -0.5)
    layout = (NB, HB, BLOCKS)
    delta_gate = expand(sign_flips[0], subspace, fast_gains[0], fast_scales[0], block_orders[0], factors[0], parts)
    delta_out = expand(sign_flips[1], subspace, fast_gains[1], fast_scales[1], block_orders[1], factors[1], parts)
    delta_gate = delta_gate.reshape(parts, D, FF // parts).transpose(1, 0, 2).reshape(D, FF)
    gate_weight = (gate_base + delta_gate).astype(jnp.bfloat16)
    out_weight = (out_base + delta_out.reshape(FF, D)).astype(jnp.bfloat16)
    gate = jnp.dot(tokens, gate_weight, preferred_element_type=jnp.float32)
    up = jnp.dot(tokens, up_base, preferred_element_type=jnp.float32)
    hidden = (gelu_tanh(gate) * up).astype(jnp.bfloat16)
    hidden_grad = contract(cotangent, out_weight, 1, 1)
    gate_grad = (hidden_grad * up * gelu_slope(gate)).astype(jnp.bfloat16)
    out_grad = contract(hidden, cotangent, 0, 0)
    in_grad = contract(tokens, gate_grad, 0, 0)
    in_grad = in_grad.reshape(D, parts, FF // parts).transpose(1, 0, 2).reshape(layout)
    out_grad = out_grad.reshape(layout)
    total = adjoint(in_grad, sign_flips[0], fast_gains[0], fast_scales[0], block_orders[0], factors[0], parts)
    total = total + adjoint(out_grad, sign_flips[1], fast_gains[1], fast_scales[1], block_orders[1], factors[1], parts)
    return total
```

```python
import jax
import jax.numpy as jnp
from jax import lax
from jax.sharding import PartitionSpec as P

D = 4096
FF = 10240


def hadamard(size, dtype):
    index = jnp.arange(size, dtype=jnp.int32)
    anded = jnp.bitwise_and(index[:, None], index[None, :])
    parity = jnp.zeros((size, size), jnp.int32)
    for bit in range(max(size.bit_length() - 1, 0)):
        parity = jnp.bitwise_xor(parity, jnp.bitwise_and(jnp.right_shift(anded, bit), 1))
    return (1 - 2 * parity).astype(dtype)


def gelu_pair(value):
    argument = 0.7978845608028654 * (value + 0.044715 * value * value * value)
    tangent = jnp.tanh(argument)
    slope = 0.5 * (1.0 + tangent) + 0.5 * value * (1.0 - tangent * tangent) * 0.7978845608028654 * (
        1.0 + 0.134145 * value * value
    )
    return 0.5 * value * (1.0 + tangent), slope


def contract(left, right, left_dim, right_dim):
    return lax.dot_general(
        left, right, (((left_dim,), (right_dim,)), ((), ())), preferred_element_type=jnp.float32
    )


def turning(order, blocks_all, parts):
    inner = blocks_all // parts
    column = jnp.arange(blocks_all, dtype=jnp.int32)[None, :]
    row = order[:, None]
    anded = jnp.bitwise_and(row // inner, column // inner)
    parity = jnp.zeros(anded.shape, jnp.int32)
    for bit in range(max(parts.bit_length() - 1, 0)):
        parity = jnp.bitwise_xor(parity, jnp.bitwise_and(jnp.right_shift(anded, bit), 1))
    return jnp.where(row % inner == column % inner, 1 - 2 * parity, 0).astype(jnp.bfloat16)


def local_spread(signs, subspace):
    inner, width, _ = signs.shape
    lifted = signs * subspace.astype(jnp.bfloat16)[:, :, None]
    lifted = jnp.einsum(
        "dc,ack->adk", hadamard(width, jnp.bfloat16), lifted, preferred_element_type=jnp.float32
    ).astype(jnp.bfloat16)
    lifted = jnp.einsum(
        "ba,ack->bck", hadamard(inner, jnp.bfloat16), lifted, preferred_element_type=jnp.float32
    )
    return (lifted * (inner * width) ** (-0.5)).astype(jnp.bfloat16)


def to_columns(item, parts):
    inner, width, vectors = item.shape
    cut = item.reshape(inner, parts, (width // parts) * vectors).transpose(1, 0, 2)
    moved = lax.all_to_all(cut, "fsdp", split_axis=0, concat_axis=0, tiled=True)
    return moved.reshape(parts * inner, (width // parts) * vectors)


def to_blocks(item, parts, vectors):
    blocks_all, wide = item.shape
    inner, some = blocks_all // parts, wide // vectors
    moved = lax.all_to_all(
        item.reshape(parts, inner, wide), "fsdp", split_axis=0, concat_axis=0, tiled=True
    )
    moved = moved.reshape(parts, inner, some, vectors).transpose(1, 0, 2, 3)
    return moved.reshape(inner, parts * some, vectors)


def middle_forward(first, gains, turn, parts):
    blocks_all = first.shape[0]
    turned = contract(turn, first, 1, 0) * parts ** (-0.5)
    mixed = (gains.astype(jnp.float32) * turned).astype(jnp.bfloat16)
    second = contract(hadamard(blocks_all, jnp.bfloat16), mixed, 1, 0)
    return (second * blocks_all ** (-0.5)).astype(jnp.bfloat16)


def middle_adjoint(back, gains, turn, parts):
    blocks_all = back.shape[0]
    spread = contract(hadamard(blocks_all, jnp.bfloat16), back, 1, 0) * blocks_all ** (-0.5)
    spread = (gains.astype(jnp.float32) * spread).astype(jnp.bfloat16)
    folded = contract(turn, spread, 0, 0)
    return (folded * parts ** (-0.5)).astype(jnp.bfloat16)


def local_finish(second, scales, factor):
    width = second.shape[1]
    wide = jnp.einsum(
        "dc,ack->adk", hadamard(width, jnp.bfloat16), second, preferred_element_type=jnp.float32
    )
    return wide * (scales[:, None, :] * (factor * width ** (-0.5)))


def local_gather_back(grads, scales, factor):
    width = grads.shape[1]
    scaled = (grads * (scales[:, None, :] * (factor * width ** (-0.5)))).astype(jnp.bfloat16)
    back = jnp.einsum(
        "dc,ack->adk", hadamard(width, jnp.bfloat16), scaled, preferred_element_type=jnp.float32
    )
    return back.astype(jnp.bfloat16)


def local_adjoint_finish(folded, signs):
    inner, width, _ = signs.shape
    wide = jnp.einsum(
        "dc,ack->adk", hadamard(width, jnp.bfloat16), folded, preferred_element_type=jnp.float32
    ).astype(jnp.bfloat16)
    wide = jnp.einsum(
        "ba,ack->bck", hadamard(inner, jnp.bfloat16), wide, preferred_element_type=jnp.float32
    )
    return jnp.sum(signs.astype(jnp.float32) * wide, axis=2) * (inner * width) ** (-0.5)


def on_device(
    tokens,
    cotangent,
    gate_base,
    up_base,
    out_base,
    subspace,
    sign_flips,
    fast_gains,
    fast_scales,
    block_orders,
):
    parts, groups = lax.axis_size("fsdp"), lax.axis_size("dp")
    mine = lax.axis_index("dp")
    _, inner, width, vectors = sign_flips.shape
    blocks_all, some = fast_gains.shape[1], fast_gains.shape[2]
    share = vectors // groups
    hidden_here = gate_base.shape[1]
    direct = hidden_here % vectors == 0
    runs = hidden_here // vectors if direct else 1
    piece = hidden_here // (runs * groups)
    owned = runs * piece

    x, dy = tokens, cotangent
    for axis in ("fsdp", "dp"):
        x = lax.all_gather(x, axis, axis=0, tiled=True)
        dy = lax.all_gather(dy, axis, axis=0, tiled=True)

    factors = (D ** (-0.5), FF ** (-0.5))
    slab = (inner, width, vectors)

    def k_slice(item):
        return lax.dynamic_slice_in_dim(item, mine * share, share, axis=item.ndim - 1)

    def hidden_columns(item):
        cut = item.reshape(item.shape[0], runs, groups, piece)
        cut = lax.dynamic_index_in_dim(cut, mine, 2, keepdims=False)
        return cut.reshape(item.shape[0], owned)

    signs = k_slice(sign_flips).astype(jnp.bfloat16)
    gains = k_slice(fast_gains).reshape(2, blocks_all, some * share)
    scales = k_slice(fast_scales)
    turns = [turning(block_orders[which], blocks_all, parts) for which in range(2)]

    def expand(which):
        first = local_spread(signs[which], subspace)
        second = middle_forward(to_columns(first, parts), gains[which], turns[which], parts)
        return local_finish(to_blocks(second, parts, share), scales[which], factors[which])

    delta_gate = expand(0)
    if direct:
        base_gate = hidden_columns(gate_base).reshape(inner, width, share)
        gate_weight = (base_gate + delta_gate).astype(jnp.bfloat16).reshape(D, owned)
    else:
        base_gate = k_slice(gate_base.reshape(slab))
        gate_weight = (base_gate + delta_gate).astype(jnp.bfloat16)
        gate_weight = lax.all_gather(gate_weight, "dp", axis=2, tiled=True)
        gate_weight = hidden_columns(gate_weight.reshape(gate_base.shape))

    strip = inner // (runs * groups)
    delta_out = expand(1).astype(jnp.bfloat16).reshape(runs, groups, strip, width, share)
    delta_out = lax.all_to_all(delta_out, "dp", split_axis=1, concat_axis=4, tiled=True)
    base_out = lax.dynamic_index_in_dim(
        out_base.reshape(runs, groups, piece, D), mine, 1, keepdims=False
    )
    out_weight = base_out.reshape(owned, D) + delta_out.reshape(owned, D)

    gate = jnp.dot(x, gate_weight, preferred_element_type=jnp.float32)
    up = jnp.dot(x, hidden_columns(up_base), preferred_element_type=jnp.float32)
    bent, slope = gelu_pair(gate)
    hidden = (bent * up).astype(jnp.bfloat16)
    hidden_grad = contract(dy, out_weight, 1, 1)
    gate_grad = (hidden_grad * up * slope).astype(jnp.bfloat16)

    out_grad = contract(hidden, dy, 0, 0).reshape(runs, strip, width, vectors)
    strips = lax.dynamic_index_in_dim(
        fast_scales[1].reshape(runs, groups, strip, vectors), mine, 1, keepdims=False
    )
    back_out = local_gather_back(
        out_grad.reshape(runs * strip, width, vectors),
        strips.reshape(runs * strip, vectors),
        factors[1],
    )
    back_out = lax.all_to_all(
        back_out.reshape(runs, 1, strip, width, vectors), "dp", split_axis=4, concat_axis=1, tiled=True
    ).reshape(inner, width, share)

    in_grad = contract(x, gate_grad, 0, 0)
    if direct:
        in_grad = in_grad.reshape(inner, width, share)
    else:
        in_grad = lax.all_gather(in_grad.astype(jnp.bfloat16), "dp", axis=1, tiled=True)
        in_grad = k_slice(in_grad.reshape(slab)).astype(jnp.float32)
    back_gate = local_gather_back(in_grad, scales[0], factors[0])

    def fold(back, which):
        folded = middle_adjoint(to_columns(back, parts), gains[which], turns[which], parts)
        return local_adjoint_finish(to_blocks(folded, parts, share), signs[which])

    result = fold(back_out, 1) + fold(back_gate, 0)
    return lax.psum(result, "dp")


def solution(mesh):
    in_specs = (
        P(("dp", "fsdp"), None),
        P(("dp", "fsdp"), None),
        P(None, "fsdp"),
        P(None, "fsdp"),
        P("fsdp", None),
        P("fsdp", None),
        P(None, "fsdp", None, None),
        P(None, None, "fsdp", None),
        P(None, "fsdp", None),
        P(),
    )
    out_specs = P("fsdp", None)
    return jax.shard_map(
        on_device, mesh=mesh, in_specs=in_specs, out_specs=out_specs, check_vma=False
    )
```

```python
import functools

import jax
import jax.numpy as jnp
from jax import lax
from jax.experimental import pallas as pl
from jax.experimental.pallas import tpu as pltpu
from jax.sharding import PartitionSpec as P

D = 4096
FF = 10240


def hadamard(size, dtype):
    index = jnp.arange(size, dtype=jnp.int32)
    anded = jnp.bitwise_and(index[:, None], index[None, :])
    parity = jnp.zeros((size, size), jnp.int32)
    for bit in range(max(size.bit_length() - 1, 0)):
        parity = jnp.bitwise_xor(parity, jnp.bitwise_and(jnp.right_shift(anded, bit), 1))
    return (1 - 2 * parity).astype(dtype)


def gelu_pair(value):
    argument = 0.7978845608028654 * (value + 0.044715 * value * value * value)
    tangent = jnp.tanh(argument)
    slope = 0.5 * (1.0 + tangent) + 0.5 * value * (1.0 - tangent * tangent) * 0.7978845608028654 * (
        1.0 + 0.134145 * value * value
    )
    return 0.5 * value * (1.0 + tangent), slope


def contract(left, right, left_dim, right_dim):
    return lax.dot_general(
        left, right, (((left_dim,), (right_dim,)), ((), ())), preferred_element_type=jnp.float32
    )


def hadamard_rows(order, size):
    anded = jnp.bitwise_and(order[:, None], jnp.arange(size, dtype=jnp.int32)[None, :])
    parity = jnp.zeros(anded.shape, jnp.int32)
    for bit in range(max(size.bit_length() - 1, 0)):
        parity = jnp.bitwise_xor(parity, jnp.bitwise_and(jnp.right_shift(anded, bit), 1))
    return (1 - 2 * parity).astype(jnp.bfloat16)


def forward_kernel(some, scale_in, scale_out, s_ref, g_ref, sub_ref, rows_ref, tall_ref, wide_ref, e_ref, u_ref):
    width = wide_ref.shape[0]
    sub = sub_ref[...]
    for at in range(some):
        lifted = s_ref[:, at * width : (at + 1) * width] * sub
        u_ref[at * width : (at + 1) * width, :] = contract(wide_ref[...], lifted, 1, 1).astype(
            jnp.bfloat16
        )
    turned = contract(u_ref[...], rows_ref[...], 1, 1) * scale_in
    mixed = (g_ref[...].astype(jnp.float32) * turned).astype(jnp.bfloat16)
    u_ref[...] = contract(mixed, tall_ref[...], 1, 0).astype(jnp.bfloat16)
    for at in range(some):
        wide = contract(u_ref[at * width : (at + 1) * width, :], wide_ref[...], 0, 0)
        e_ref[:, at * width : (at + 1) * width] = (wide * scale_out).astype(jnp.bfloat16)


def adjoint_kernel(some, scale_out, b_ref, s_ref, g_ref, rows_ref, tall_ref, wide_ref, sum_ref, u_ref):
    width = wide_ref.shape[0]

    @pl.when(pl.program_id(0) == 0)
    def _():
        sum_ref[...] = jnp.zeros_like(sum_ref)

    for at in range(some):
        u_ref[at * width : (at + 1) * width, :] = contract(
            wide_ref[...], b_ref[:, at * width : (at + 1) * width], 1, 1
        ).astype(jnp.bfloat16)
    spread = contract(u_ref[...], tall_ref[...], 1, 0)
    spread = (g_ref[...].astype(jnp.float32) * spread).astype(jnp.bfloat16)
    u_ref[...] = contract(spread, rows_ref[...], 1, 0).astype(jnp.bfloat16)
    total = jnp.zeros(sum_ref.shape, jnp.float32)
    for at in range(some):
        wide = contract(u_ref[at * width : (at + 1) * width, :], wide_ref[...], 0, 0)
        total += s_ref[:, at * width : (at + 1) * width].astype(jnp.float32) * wide
    sum_ref[...] += total * scale_out


def vectors_at_once(count):
    return max(some for some in range(1, 6) if count % some == 0)


def chain(kernel, operands, whole, result, width, blocks_all, count, summed):
    some = vectors_at_once(count)
    flat = pl.BlockSpec((blocks_all, some * width), lambda i: (0, i))
    turned = pl.BlockSpec((some * width, blocks_all), lambda i: (i, 0))
    specs = [flat if item.shape[0] == blocks_all else turned for item in operands]
    specs += [pl.BlockSpec(item.shape, lambda i: (0, 0)) for item in whole]
    flops = 2 * count * width * blocks_all * (2 * blocks_all + 2 * width)
    return pl.pallas_call(
        functools.partial(kernel, some),
        grid=(count // some,),
        in_specs=specs,
        out_specs=pl.BlockSpec((blocks_all, width), lambda i: (0, 0)) if summed else flat,
        out_shape=result,
        scratch_shapes=[pltpu.VMEM((some * width, blocks_all), jnp.bfloat16)],
        compiler_params=pltpu.CompilerParams(vmem_limit_bytes=40 * 1024 * 1024),
        cost_estimate=pl.CostEstimate(
            flops=flops, bytes_accessed=6 * count * width * blocks_all, transcendentals=0
        ),
    )(*operands, *whole)


def exchange(item):
    return lax.all_to_all(item, "fsdp", split_axis=0, concat_axis=0, tiled=True)


def on_device(
    tokens,
    cotangent,
    gate_base,
    up_base,
    out_base,
    subspace,
    sign_flips,
    fast_gains,
    fast_scales,
    block_orders,
):
    parts, groups = lax.axis_size("fsdp"), lax.axis_size("dp")
    mine = lax.axis_index("dp")
    _, inner, width, vectors = sign_flips.shape
    blocks_all, some = fast_gains.shape[1], fast_gains.shape[2]
    share = vectors // groups
    hidden_here = gate_base.shape[1]
    direct = hidden_here % vectors == 0
    runs = hidden_here // vectors if direct else 1
    piece = hidden_here // (runs * groups)
    owned = runs * piece

    factors = (D ** (-0.5), FF ** (-0.5))
    slab = (inner, width, vectors)

    def k_slice(item):
        return lax.dynamic_slice_in_dim(item, mine * share, share, axis=item.ndim - 1)

    def hidden_columns(item):
        cut = item.reshape(item.shape[0], runs, groups, piece)
        cut = lax.dynamic_index_in_dim(cut, mine, 2, keepdims=False)
        return cut.reshape(item.shape[0], owned)

    count = -(-share // parts)
    wide_h, tall_h = hadamard(width, jnp.bfloat16), hadamard(blocks_all, jnp.bfloat16)
    rows_h = [hadamard_rows(block_orders[which], blocks_all) for which in range(2)]
    sub_all = lax.all_gather(subspace.astype(jnp.bfloat16), "fsdp", axis=0, tiled=True)

    def filled(item):
        if count * parts == share:
            return item
        return jnp.pad(item, ((0, 0), (0, 0), (0, count * parts - share)))

    def signs_to_owners(which):
        item = filled(k_slice(sign_flips[which]).astype(jnp.bfloat16))
        item = item.reshape(inner, width, parts, count).transpose(2, 0, 3, 1)
        return exchange(item.reshape(parts, inner, count * width)).reshape(blocks_all, count * width)

    def gains_to_owners(which):
        item = filled(k_slice(fast_gains[which])).reshape(blocks_all, some, parts, count)
        item = exchange(item.transpose(2, 3, 1, 0))
        return item.transpose(1, 0, 2, 3).reshape(count * width, blocks_all)

    def weights_home(item):
        item = exchange(item.reshape(parts, inner, count * width))
        item = item.reshape(parts, inner, count, width).transpose(1, 3, 0, 2)
        return item.reshape(inner, width, parts * count)[:, :, :share]

    def grads_to_owners(item):
        item = filled(item).reshape(inner, width, parts, count).transpose(2, 0, 3, 1)
        return exchange(item.reshape(parts, inner, count * width)).reshape(blocks_all, count * width)

    def expand(which):
        return chain(
            lambda some, *refs: forward_kernel(
                some,
                (blocks_all * width) ** (-0.5),
                (blocks_all * width) ** (-0.5),
                *refs,
            ),
            (signs[which], gains[which]),
            (sub_all, rows_h[which], tall_h, wide_h),
            jax.ShapeDtypeStruct((blocks_all, count * width), jnp.bfloat16),
            width,
            blocks_all,
            count,
            False,
        )

    gains_0 = gains_to_owners(0)
    signs_0 = signs_to_owners(0)
    gains_1 = gains_to_owners(1)
    signs_1 = signs_to_owners(1)
    signs, gains = (signs_0, signs_1), (gains_0, gains_1)

    x = lax.all_gather(tokens, "fsdp", axis=0, tiled=True)
    dy = lax.all_gather(cotangent, "fsdp", axis=0, tiled=True)
    x, dy, sub_all, gains_0 = lax.optimization_barrier((x, dy, sub_all, gains_0))
    gains = (gains_0, gains_1)
    x = lax.all_gather(x, "dp", axis=0, tiled=True)
    dy = lax.all_gather(dy, "dp", axis=0, tiled=True)

    def scaled_home(which):
        own = k_slice(fast_scales[which])[:, None, :] * factors[which]
        return weights_home(expand(which)).astype(jnp.float32) * own

    delta_gate = scaled_home(0)
    if direct:
        base_gate = hidden_columns(gate_base).reshape(inner, width, share)
        gate_weight = (base_gate + delta_gate).astype(jnp.bfloat16).reshape(D, owned)
    else:
        base_gate = k_slice(gate_base.reshape(slab))
        gate_weight = (base_gate + delta_gate).astype(jnp.bfloat16)
        gate_weight = lax.all_gather(gate_weight, "dp", axis=2, tiled=True)
        gate_weight = hidden_columns(gate_weight.reshape(gate_base.shape))

    strip = inner // (runs * groups)
    delta_out = scaled_home(1).astype(jnp.bfloat16).reshape(runs, groups, strip, width, share)
    delta_out = lax.all_to_all(delta_out, "dp", split_axis=1, concat_axis=4, tiled=True)
    base_out = lax.dynamic_index_in_dim(
        out_base.reshape(runs, groups, piece, D), mine, 1, keepdims=False
    )
    out_weight = base_out.reshape(owned, D) + delta_out.reshape(owned, D)

    gate = jnp.dot(x, gate_weight, preferred_element_type=jnp.float32)
    up = jnp.dot(x, hidden_columns(up_base), preferred_element_type=jnp.float32)
    bent, slope = gelu_pair(gate)
    hidden = (bent * up).astype(jnp.bfloat16)
    hidden_grad = contract(dy, out_weight, 1, 1)
    gate_grad = (hidden_grad * up * slope).astype(jnp.bfloat16)

    out_grad = contract(hidden, dy, 0, 0).reshape(runs, strip, width, vectors)
    back_factor = (blocks_all * width) ** (-0.5)
    strips = lax.dynamic_index_in_dim(
        fast_scales[1].reshape(runs, groups, strip, vectors), mine, 1, keepdims=False
    )
    back_out = (out_grad * (strips[:, :, None, :] * (factors[1] * back_factor))).astype(jnp.bfloat16)
    back_out = lax.all_to_all(
        back_out.reshape(runs, 1, strip, width, vectors), "dp", split_axis=4, concat_axis=1, tiled=True
    ).reshape(inner, width, share)

    in_grad = contract(x, gate_grad, 0, 0)
    if direct:
        in_grad = in_grad.reshape(inner, width, share)
    else:
        in_grad = lax.all_gather(in_grad.astype(jnp.bfloat16), "dp", axis=1, tiled=True)
        in_grad = k_slice(in_grad.reshape(slab)).astype(jnp.float32)
    own = k_slice(fast_scales[0])[:, None, :] * (factors[0] * back_factor)
    back_gate = (in_grad * own).astype(jnp.bfloat16)

    def fold(back, which):
        return chain(
            lambda some, *refs: adjoint_kernel(some, (blocks_all * width) ** (-0.5), *refs),
            (grads_to_owners(back), signs[which], gains[which]),
            (rows_h[which], tall_h, wide_h),
            jax.ShapeDtypeStruct((blocks_all, width), jnp.float32),
            width,
            blocks_all,
            count,
            True,
        )

    result = fold(back_out, 1) + fold(back_gate, 0)
    result = lax.psum_scatter(result, "fsdp", scatter_dimension=0, tiled=True)
    return lax.psum(result, "dp")


def solution(mesh):
    in_specs = (
        P(("dp", "fsdp"), None),
        P(("dp", "fsdp"), None),
        P(None, "fsdp"),
        P(None, "fsdp"),
        P("fsdp", None),
        P("fsdp", None),
        P(None, "fsdp", None, None),
        P(None, None, "fsdp", None),
        P(None, "fsdp", None),
        P(),
    )
    out_specs = P("fsdp", None)
    return jax.shard_map(
        on_device, mesh=mesh, in_specs=in_specs, out_specs=out_specs, check_vma=False
    )
```

```python
import functools

import jax
import jax.numpy as jnp
from jax import lax
from jax.experimental import pallas as pl
from jax.experimental.pallas import tpu as pltpu
from jax.sharding import PartitionSpec as P

D = 4096
FF = 10240


def hadamard(size, dtype):
    index = jnp.arange(size, dtype=jnp.int32)
    anded = jnp.bitwise_and(index[:, None], index[None, :])
    parity = jnp.zeros((size, size), jnp.int32)
    for bit in range(max(size.bit_length() - 1, 0)):
        parity = jnp.bitwise_xor(parity, jnp.bitwise_and(jnp.right_shift(anded, bit), 1))
    return (1 - 2 * parity).astype(dtype)


def gelu_pair(value):
    argument = 0.7978845608028654 * (value + 0.044715 * value * value * value)
    tangent = jnp.tanh(argument)
    slope = 0.5 * (1.0 + tangent) + 0.5 * value * (1.0 - tangent * tangent) * 0.7978845608028654 * (
        1.0 + 0.134145 * value * value
    )
    return 0.5 * value * (1.0 + tangent), slope


def contract(left, right, left_dim, right_dim):
    return lax.dot_general(
        left, right, (((left_dim,), (right_dim,)), ((), ())), preferred_element_type=jnp.float32
    )


def hadamard_rows(order, size):
    anded = jnp.bitwise_and(order[:, None], jnp.arange(size, dtype=jnp.int32)[None, :])
    parity = jnp.zeros(anded.shape, jnp.int32)
    for bit in range(max(size.bit_length() - 1, 0)):
        parity = jnp.bitwise_xor(parity, jnp.bitwise_and(jnp.right_shift(anded, bit), 1))
    return (1 - 2 * parity).astype(jnp.bfloat16)


def load_vector(ref, at):
    parts, _, inner, width = ref.shape
    item = ref[:, at]
    if inner % 16:
        return item.astype(jnp.float32).reshape(parts * inner, width).astype(item.dtype)
    return item.reshape(parts * inner, width)


def forward_kernel(some, scale_in, scale_out, s_ref, g_ref, sub_ref, rows_ref, tall_ref, wide_ref, e_ref, u_ref):
    width = wide_ref.shape[0]
    sub = sub_ref[...]
    for at in range(some):
        lifted = load_vector(s_ref, at) * sub
        u_ref[at * width : (at + 1) * width, :] = contract(wide_ref[...], lifted, 1, 1).astype(
            jnp.bfloat16
        )
    turned = contract(u_ref[...], rows_ref[...], 1, 1) * scale_in
    mixed = (g_ref[...].astype(jnp.float32) * turned).astype(jnp.bfloat16)
    u_ref[...] = contract(mixed, tall_ref[...], 1, 0).astype(jnp.bfloat16)
    for at in range(some):
        wide = contract(u_ref[at * width : (at + 1) * width, :], wide_ref[...], 0, 0)
        wide = (wide * scale_out).reshape(e_ref.shape[0], *e_ref.shape[2:])
        e_ref[:, at] = wide.astype(jnp.bfloat16)


def adjoint_kernel(some, scale_out, b_ref, s_ref, g_ref, rows_ref, tall_ref, wide_ref, sum_ref, u_ref):
    width = wide_ref.shape[0]

    @pl.when(pl.program_id(0) == 0)
    def _():
        sum_ref[...] = jnp.zeros_like(sum_ref)

    for at in range(some):
        u_ref[at * width : (at + 1) * width, :] = contract(
            wide_ref[...], load_vector(b_ref, at), 1, 1
        ).astype(jnp.bfloat16)
    spread = contract(u_ref[...], tall_ref[...], 1, 0)
    spread = (g_ref[...].astype(jnp.float32) * spread).astype(jnp.bfloat16)
    u_ref[...] = contract(spread, rows_ref[...], 1, 0).astype(jnp.bfloat16)
    total = jnp.zeros(sum_ref.shape, jnp.float32)
    for at in range(some):
        wide = contract(u_ref[at * width : (at + 1) * width, :], wide_ref[...], 0, 0)
        total += load_vector(s_ref, at).astype(jnp.float32) * wide
    sum_ref[...] += total * scale_out


def vectors_at_once(count):
    return max(some for some in range(1, 6) if count % some == 0)


def chain(kernel, operands, whole, result, width, blocks_all, count, summed):
    some = vectors_at_once(count)
    parts = next(item.shape[0] for item in operands if item.ndim == 4)
    flat = pl.BlockSpec((parts, some, blocks_all // parts, width), lambda i: (0, i, 0, 0))
    turned = pl.BlockSpec((some * width, blocks_all), lambda i: (i, 0))
    specs = [flat if item.ndim == 4 else turned for item in operands]
    specs += [pl.BlockSpec(item.shape, lambda i: (0, 0)) for item in whole]
    flops = 2 * count * width * blocks_all * (2 * blocks_all + 2 * width)
    return pl.pallas_call(
        functools.partial(kernel, some),
        grid=(count // some,),
        in_specs=specs,
        out_specs=pl.BlockSpec((blocks_all, width), lambda i: (0, 0)) if summed else flat,
        out_shape=result,
        scratch_shapes=[pltpu.VMEM((some * width, blocks_all), jnp.bfloat16)],
        compiler_params=pltpu.CompilerParams(vmem_limit_bytes=40 * 1024 * 1024),
        cost_estimate=pl.CostEstimate(
            flops=flops, bytes_accessed=6 * count * width * blocks_all, transcendentals=0
        ),
    )(*operands, *whole)


def exchange(item):
    return lax.all_to_all(item, "fsdp", split_axis=0, concat_axis=0, tiled=True)


def on_device(
    tokens,
    cotangent,
    gate_base,
    up_base,
    out_base,
    subspace,
    sign_flips,
    fast_gains,
    fast_scales,
    block_orders,
):
    parts, groups = lax.axis_size("fsdp"), lax.axis_size("dp")
    mine = lax.axis_index("dp")
    _, inner, width, vectors = sign_flips.shape
    blocks_all, some = fast_gains.shape[1], fast_gains.shape[2]
    share = vectors // groups
    hidden_here = gate_base.shape[1]
    direct = hidden_here % vectors == 0
    runs = hidden_here // vectors if direct else 1
    piece = hidden_here // (runs * groups)
    owned = runs * piece

    factors = (D ** (-0.5), FF ** (-0.5))
    slab = (inner, width, vectors)

    def k_slice(item):
        return lax.dynamic_slice_in_dim(item, mine * share, share, axis=item.ndim - 1)

    def of_matrix(item, which):
        start = (which, 0, 0, mine * share)
        return lax.dynamic_slice(item, start, (1,) + item.shape[1:3] + (share,))[0]

    def hidden_columns(item):
        cuts = [
            lax.dynamic_slice_in_dim(item, run * vectors + mine * piece, piece, axis=1)
            for run in range(runs)
        ]
        return jnp.concatenate(cuts, axis=1) if runs > 1 else cuts[0]

    count = -(-share // parts)
    wide_h, tall_h = hadamard(width, jnp.bfloat16), hadamard(blocks_all, jnp.bfloat16)
    rows_h = [hadamard_rows(block_orders[which], blocks_all) for which in range(2)]
    sub_all = exchange(
        jnp.broadcast_to(subspace.astype(jnp.bfloat16), (parts, inner, width))
    ).reshape(blocks_all, width)

    def filled(item, axis):
        if count * parts == share:
            return item
        sides = [(0, 0)] * item.ndim
        sides[axis] = (0, count * parts - share)
        return jnp.pad(item, sides)

    def to_owners(item):
        return exchange(filled(item, 0).reshape(parts, count, inner, width))

    def sign_payload(which):
        return of_matrix(sign_flips, which).astype(jnp.bfloat16).transpose(2, 0, 1)

    def gains_to_owners(which):
        item = filled(of_matrix(fast_gains, which), 2).reshape(blocks_all, some, parts, count)
        item = exchange(item.transpose(2, 3, 1, 0))
        return item.transpose(1, 0, 2, 3).reshape(count * width, blocks_all)

    def weights_home(item):
        return exchange(item).reshape(parts * count, inner, width)[:share]

    def expand(which, signs, gains):
        return chain(
            lambda some, *refs: forward_kernel(
                some,
                (blocks_all * width) ** (-0.5),
                (blocks_all * width) ** (-0.5),
                *refs,
            ),
            (signs, gains),
            (sub_all, rows_h[which], tall_h, wide_h),
            jax.ShapeDtypeStruct((parts, count, inner, width), jnp.bfloat16),
            width,
            blocks_all,
            count,
            False,
        )

    def scaled(item, which):
        own = k_slice(fast_scales[which]).T[:, :, None] * factors[which]
        return (item.astype(jnp.float32) * own).astype(jnp.bfloat16)

    gains_0 = gains_to_owners(0)
    signs_0 = to_owners(sign_payload(0))
    payload, gains_0 = lax.optimization_barrier((sign_payload(1), gains_0))
    gains_1 = gains_to_owners(1)
    home_0 = weights_home(expand(0, signs_0, gains_0))

    x = lax.all_gather(tokens, "fsdp", axis=0, tiled=True)
    dy = lax.all_gather(cotangent, "fsdp", axis=0, tiled=True)
    x, dy, gains_1 = lax.optimization_barrier((x, dy, gains_1))
    x = lax.all_gather(x, "dp", axis=0, tiled=True)
    dy = lax.all_gather(dy, "dp", axis=0, tiled=True)

    up_own = hidden_columns(up_base)
    gate_own = hidden_columns(gate_base) if direct else gate_base
    out_own = lax.dynamic_index_in_dim(
        out_base.reshape(runs, groups, piece, D), mine, 1, keepdims=False
    ).reshape(owned, D)
    payload, home_0, up_own, gate_own, out_own = lax.optimization_barrier(
        (payload, home_0, up_own, gate_own, out_own)
    )
    signs_1 = to_owners(payload)

    delta_gate = scaled(home_0, 0).transpose(1, 2, 0)
    if direct:
        gate_weight = gate_own + delta_gate.reshape(D, owned)
    else:
        delta_gate = lax.all_gather(delta_gate, "dp", axis=2, tiled=True)
        gate_weight = hidden_columns(gate_own + delta_gate.reshape(gate_own.shape))
    gate_weight, signs_1 = lax.optimization_barrier((gate_weight, signs_1))
    signs, gains = (signs_0, signs_1), (gains_0, gains_1)

    strip = inner // (runs * groups)
    home_1 = weights_home(expand(1, signs_1, gains_1))

    gate = jnp.dot(x, gate_weight, preferred_element_type=jnp.float32)
    up = jnp.dot(x, up_own, preferred_element_type=jnp.float32)
    bent, slope = gelu_pair(gate)
    hidden = (bent * up).astype(jnp.bfloat16)
    back_factor = (blocks_all * width) ** (-0.5)
    strips = lax.dynamic_index_in_dim(
        fast_scales[1].reshape(runs, groups, strip, vectors), mine, 1, keepdims=False
    ).reshape(runs * strip, vectors)
    out_grad = contract(hidden, dy, 0, 0).astype(jnp.bfloat16)
    out_grad = out_grad.reshape(runs * strip, width, vectors).transpose(2, 0, 1)
    out_grad = out_grad.astype(jnp.float32) * (strips.T[:, :, None] * (factors[1] * back_factor))
    out_grad = out_grad.astype(jnp.bfloat16)
    home_1, out_grad = lax.optimization_barrier((home_1, out_grad))
    back_out = lax.all_to_all(
        out_grad.reshape(groups, share, runs, strip, width), "dp", split_axis=0, concat_axis=0, tiled=True
    )
    back_out = back_out.transpose(1, 2, 0, 3, 4).reshape(share, inner, width)

    delta_out = scaled(home_1, 1).reshape(share, runs, groups, strip, width)
    delta_out = lax.all_to_all(
        delta_out.transpose(2, 0, 1, 3, 4), "dp", split_axis=0, concat_axis=0, tiled=True
    )
    delta_out = delta_out.reshape(vectors, runs * strip, width).transpose(1, 2, 0)
    out_weight = out_own + delta_out.reshape(owned, D)
    hidden_grad = contract(dy, out_weight, 1, 1)
    gate_grad = (hidden_grad * up * slope).astype(jnp.bfloat16)

    in_grad = contract(x, gate_grad, 0, 0).astype(jnp.bfloat16)
    if direct:
        in_grad = in_grad.reshape(inner, width, share)
    else:
        in_grad = lax.all_gather(in_grad, "dp", axis=1, tiled=True)
        in_grad = k_slice(in_grad.reshape(slab))
    back_gate = scaled(in_grad.transpose(2, 0, 1), 0) * jnp.bfloat16(back_factor)

    def fold(back, which):
        return chain(
            lambda some, *refs: adjoint_kernel(some, (blocks_all * width) ** (-0.5), *refs),
            (to_owners(back), signs[which], gains[which]),
            (rows_h[which], tall_h, wide_h),
            jax.ShapeDtypeStruct((blocks_all, width), jnp.float32),
            width,
            blocks_all,
            count,
            True,
        )

    result = fold(back_out, 1) + fold(back_gate, 0)
    result = jnp.sum(exchange(result.reshape(parts, inner, width)), axis=0)
    return lax.psum(result, "dp")


def solution(mesh):
    in_specs = (
        P(("dp", "fsdp"), None),
        P(("dp", "fsdp"), None),
        P(None, "fsdp"),
        P(None, "fsdp"),
        P("fsdp", None),
        P("fsdp", None),
        P(None, "fsdp", None, None),
        P(None, None, "fsdp", None),
        P(None, "fsdp", None),
        P(),
    )
    out_specs = P("fsdp", None)
    return jax.shard_map(
        on_device, mesh=mesh, in_specs=in_specs, out_specs=out_specs, check_vma=False
    )
```
